128 devices in a mesh: vocab: 16 (over x, z), tok: 8 (over y, core).
Axes of the slice: x: 4, y: 4, z: 4, core: 2. Of those that a mesh axis runs over, the one named last changes fastest.
Arguments:
- hidden_states: bfloat16 [1024, 2048], P('tok'), may hold values from -8 to 8, as said below
- tied_table: bfloat16 [131072, 2048], P(('vocab', 'tok')), may hold values from -3 to 3
- labels: int32 [1024], P('tok'), may hold values from 0 to 131071
- dec_ids: int32 [1024], P('tok'), may hold values from 0 to 131071
- enc_ids: int32 [1024], P('tok'), may hold values from 0 to 131071
- dec_grad: bfloat16 [1024, 2048], P('tok'), may hold values from -6 to 6
- enc_grad: bfloat16 [1024, 2048], P('tok'), may hold values from -6 to 6
Outputs:
- grad_table: float32 [131072, 2048], P(('vocab', 'tok'))
- grad_hidden: float32 [1024, 2048], P('tok', 'vocab')
- token_loss: float32 [1024], P('tok')
The draws below stay inside these ranges and needn't reach their ends.
Inputs may be any that keep to these rules, and one draw needn't show every extreme that they name: `hidden_states`: decoder states, of order one.
All inputs are finite; a program needn't handle non-finite values.
Results may differ from the reference program's by a relative error of at most 0.002.
Values may be sent and summed in bfloat16 or wider, within the bound.
No kernel may reach another device: no remote copies, remote signals or barrier semaphores. Data moves between devices by JAX's collectives and lax.ppermute only.
A program may use at most 128 MiB of HBM per device.

```python
import math
import jax
import jax.numpy as jnp
import numpy as np

D = 2048
VOCAB = 131072
TOKENS = 1024


def draw_hidden_states(key, part):
    key = jax.random.fold_in(key, 1)
    values = jnp.clip(jax.random.normal(key, (TOKENS, D), jnp.float32), -6.0, 6.0)
    return values.astype(jnp.bfloat16)


def draw_tied_table(key, part):
    key = jax.random.fold_in(key, 2)
    spread = 3.2 / math.sqrt(D)
    values = jnp.clip(jax.random.normal(key, (VOCAB, D), jnp.float32), -6.0, 6.0) * spread
    return values.astype(jnp.bfloat16)


def with_ends(result, own_key, least, high):
    spot = [jax.random.randint(jax.random.fold_in(own_key, axis), (), 0, length) for axis, length in enumerate(result.shape)]
    main_axis = result.shape.index(max(result.shape))
    neighbour = spot[:main_axis] + [(spot[main_axis] + 1) % result.shape[main_axis]] + spot[main_axis + 1:]
    return result.at[tuple(spot)].set(least).at[tuple(neighbour)].set(high)


def level_of(key, shape, cuts, low, largest):
    level, own = 1.0, jax.random.fold_in(key, 6)
    for dim, parts in cuts:
        draws = jnp.exp(jax.random.uniform(jax.random.fold_in(own, dim), (parts,), jnp.float32, low / len(cuts), largest / len(cuts)))
        level = level * jnp.repeat(draws, shape[dim] // parts).reshape([-1 if axis == dim else 1 for axis in range(len(shape))])
    return level


def ranked_wide(key, dims, count, skew):
    loads = [min(1 << octave, count + 1 - (1 << octave)) * (1 << 20) // math.isqrt((1 << octave) ** skew) + 1 for octave in range((count + 1).bit_length()) if 1 << octave <= count]
    scale = 1 + sum(loads) // (1 << 30)
    table = np.cumsum(np.array([max(1, weight // scale) for weight in loads]))
    ticket = jax.random.randint(jax.random.fold_in(key, 1), dims, 0, int(table[len(loads) - 1]))
    start = jnp.left_shift(1, jnp.searchsorted(jnp.asarray(table, jnp.int32), ticket, side="right").astype(jnp.int32))
    grade = start - 1 + jax.random.randint(jax.random.fold_in(key, 4), dims, 0, 1 << 30) % jnp.minimum(start, count + 1 - start)
    return jax.random.permutation(jax.random.fold_in(key, 2), count)[grade].astype(jnp.int32)


def centred(key, dims, width, reach, pieces=(), kind=jnp.bfloat16):
    level = level_of(key, dims, pieces, -0.22, 0.18) if pieces else 1.0
    values = jax.random.normal(key, dims, jnp.float32) * width * level
    return jnp.minimum(jnp.maximum(values, -reach), reach).astype(kind)


def setup_inputs(seed: int = 0) -> dict:
    key_list = jax.random.split(jax.random.key(seed), 8)
    hidden_states = draw_hidden_states(jax.random.fold_in(key_list[7], 71), 0)
    tied_table = draw_tied_table(jax.random.fold_in(key_list[7], 71), 0)
    labels = with_ends(ranked_wide(key_list[2], (TOKENS,), VOCAB, 2), jax.random.fold_in(key_list[2], 3), 0, VOCAB - 1).astype(jnp.int32)
    dec_ids = with_ends(ranked_wide(key_list[3], (TOKENS,), VOCAB, 1), jax.random.fold_in(key_list[3], 3), 0, VOCAB - 1).astype(jnp.int32)
    enc_ids = with_ends(ranked_wide(key_list[4], (TOKENS,), VOCAB, 1), jax.random.fold_in(key_list[4], 3), 0, VOCAB - 1).astype(jnp.int32)
    dec_grad = centred(key_list[5], (TOKENS, D), 1.0, 6.0, ((0, 8),))
    enc_grad = centred(key_list[6], (TOKENS, D), 1.0, 6.0, ((0, 8),))
    return dict(hidden_states=hidden_states, tied_table=tied_table, labels=labels, dec_ids=dec_ids, enc_ids=enc_ids, dec_grad=dec_grad, enc_grad=enc_grad)


def reference(hidden_states, tied_table, labels, dec_ids, enc_ids, dec_grad, enc_grad):
    logits = jnp.dot(hidden_states, tied_table.T, preferred_element_type=jnp.float32)
    highest = jnp.max(logits, axis=1)
    totals = jnp.sum(jnp.exp(logits - highest[:, None]), axis=1)
    log_norm = highest + jnp.log(totals)
    columns = jnp.arange(VOCAB, dtype=jnp.int32)
    is_label = labels[:, None] == columns[None, :]
    picked = jnp.sum(jnp.where(is_label, logits, jnp.zeros_like(logits)), axis=1)
    token_loss = log_norm - picked
    logit_grad = (jnp.exp(logits - log_norm[:, None]) - is_label.astype(jnp.float32)).astype(jnp.bfloat16)
    grad_hidden = jnp.dot(logit_grad, tied_table, preferred_element_type=jnp.float32)
    grad_table = jnp.dot(logit_grad.T, hidden_states, preferred_element_type=jnp.float32)
    grad_table = grad_table.at[dec_ids].add(dec_grad.astype(jnp.float32))
    grad_table = grad_table.at[enc_ids].add(enc_grad.astype(jnp.float32))
    return grad_table, grad_hidden, token_loss
```

```python
import functools

import jax
import jax.numpy as jnp
from jax import lax
from jax.experimental import pallas as pl
from jax.experimental.pallas import tpu as pltpu
from jax.sharding import PartitionSpec as P

BF = jnp.bfloat16
F32 = jnp.float32
SLOTS = 16
HOPS = (0, 1, 3, 2)


def along_y(x, hop):
    pairs = [(t, ((t // 2 - hop) % 4) * 2 + t % 2) for t in range(8)]
    return lax.ppermute(x, "tok", pairs)


def along_z(x, hop):
    pairs = [(v, (v // 4) * 4 + (v % 4 - hop) % 4) for v in range(16)]
    return lax.ppermute(x, "vocab", pairs)


def along_x(x, hop):
    pairs = [(v, (v - 4 * hop) % 16) for v in range(16)]
    return lax.ppermute(x, "vocab", pairs)


def sibling(x):
    return lax.ppermute(x, "tok", [(t, t ^ 1) for t in range(8)])


def logits_kernel(n, *refs):
    hidden = refs[:n]
    own_ref, sib_ref, label_ref = refs[n : n + 3]
    logits_ref, stats_ref = refs[n + 3 : n + 5]
    grads = refs[n + 5 : 2 * n + 5]
    states, peak, total, picked, acc = refs[2 * n + 5 :]
    phase, step = pl.program_id(0), pl.program_id(1)
    steps = pl.num_programs(1)
    half = steps // 2
    rows = own_ref.shape[0]

    @pl.when((phase == 0) & (step == 0))
    def _():
        for i in range(n):
            states[128 * i : 128 * (i + 1), :] = hidden[i][...]
        peak[...] = jnp.full_like(peak, -jnp.inf)

    def forward(table):
        part = lax.dot_general(
            states[...], table[...], (((1,), (1,)), ((), ())), preferred_element_type=F32
        )
        logits_ref[step] = part
        peak[...] = jnp.maximum(peak[...], jnp.max(part, axis=1, keepdims=True))

    def backward(table, label, first):
        part = logits_ref[step]
        column = lax.broadcasted_iota(jnp.int32, part.shape, 1) + first
        is_label = column == label
        weight = jnp.exp(part - peak[...])
        row_sum = jnp.sum(weight, axis=1, keepdims=True)
        hit = jnp.sum(jnp.where(is_label, part, 0.0), axis=1, keepdims=True)
        masked = jnp.where(is_label, 0.0, weight).astype(BF)
        grad = jnp.dot(masked, table[...], preferred_element_type=F32)

        @pl.when(step == 0)
        def _():
            total[...] = row_sum
            picked[...] = hit
            acc[...] = grad

        @pl.when(step > 0)
        def _():
            total[...] += row_sum
            picked[...] += hit
            acc[...] += grad

    @pl.when((phase == 0) & (step < half))
    def _():
        forward(own_ref)

    @pl.when((phase == 0) & (step >= half))
    def _():
        forward(sib_ref)

    @pl.when((phase == 1) & (step < half))
    def _():
        backward(own_ref, label_ref[:, 0:1], step * rows)

    @pl.when((phase == 1) & (step >= half))
    def _():
        backward(sib_ref, label_ref[:, 1:2], (step - half) * rows)

    @pl.when((phase == 1) & (step == steps - 1))
    def _():
        for i in range(n):
            grads[i][...] = acc[128 * i : 128 * (i + 1), :].astype(BF)
        lane = lax.broadcasted_iota(jnp.int32, (128 * n, 128), 1)
        both = jnp.where(
            lane == 0, peak[...], jnp.where(lane == 1, total[...], jnp.where(lane == 2, picked[...], 0.0))
        )
        stats_ref[...] = both.T[0:8, :]


def logits_and_grads(hidden, own, sib, labels):
    n, width, chunk = len(hidden), own.shape[1], 512
    count = own.shape[0] // chunk
    tokens = 128 * n

    def whole(*shape):
        return pl.BlockSpec(shape, lambda p, j: (0,) * len(shape), pipeline_mode=pl.Buffered(1))

    return pl.pallas_call(
        functools.partial(logits_kernel, n),
        grid=(2, 2 * count),
        in_specs=[whole(128, width)] * n
        + [
            pl.BlockSpec((chunk, width), lambda p, j: (jnp.minimum(j, count - 1), 0)),
            pl.BlockSpec((chunk, width), lambda p, j: (jnp.maximum(j - count, 0), 0)),
            whole(tokens, 2),
        ],
        out_specs=[
            pl.BlockSpec((2 * count, tokens, chunk), lambda p, j: (0, 0, 0)),
            pl.BlockSpec((8, tokens), lambda p, j: (0, 0)),
        ]
        + [pl.BlockSpec((128, width), lambda p, j: (0, 0))] * n,
        out_shape=[
            jax.ShapeDtypeStruct((2 * count, tokens, chunk), F32),
            jax.ShapeDtypeStruct((8, tokens), F32),
        ]
        + [jax.ShapeDtypeStruct((128, width), BF)] * n,
        scratch_shapes=[
            pltpu.VMEM((tokens, width), BF),
            pltpu.VMEM((tokens, 1), F32),
            pltpu.VMEM((tokens, 1), F32),
            pltpu.VMEM((tokens, 1), F32),
            pltpu.VMEM((tokens, width), F32),
        ],
        compiler_params=pltpu.CompilerParams(vmem_limit_bytes=48 << 20),
        cost_estimate=pl.CostEstimate(
            flops=4 * tokens * 4 * chunk * width, bytes_accessed=16 << 20, transcendentals=tokens * 4 * chunk
        ),
    )(*hidden, own, sib, labels)


def table_kernel(p_own, p_sib, h0, h1, h2, h3, h_sib, extra, at_ref, out_ref, states):
    @pl.when(pl.program_id(0) == 0)
    def _():
        for i, h in enumerate((h0, h1, h2, h3)):
            states[128 * i : 128 * (i + 1), :] = h[...]

    dims = (((0,), (0,)), ((), ()))
    rows = out_ref.shape[0]
    row = lax.broadcasted_iota(jnp.int32, (rows, extra.shape[0]), 0) + pl.program_id(0) * rows
    named = jnp.where(row == at_ref[...], 1.0, 0.0).astype(BF)
    out = lax.dot_general(p_own[...], states[...], dims, preferred_element_type=F32)
    out += lax.dot_general(p_sib[...], h_sib[...], dims, preferred_element_type=F32)
    out += jnp.dot(named, extra[...], preferred_element_type=F32)
    out_ref[...] = out


def table_gradient(p_own, p_sib, hidden, h_sib, extra, at):
    tokens, rows = p_own.shape
    width, tile, slots = h_sib.shape[1], 256, extra.shape[0]

    def whole(*shape):
        return pl.BlockSpec(shape, lambda j: (0, 0), pipeline_mode=pl.Buffered(1))

    return pl.pallas_call(
        table_kernel,
        grid=(rows // tile,),
        in_specs=[pl.BlockSpec((tokens, tile), lambda j: (0, j))] * 2
        + [whole(128, width)] * 4
        + [whole(tokens, width), whole(slots, width), whole(1, slots)],
        out_specs=pl.BlockSpec((tile, width), lambda j: (j, 0)),
        out_shape=jax.ShapeDtypeStruct((rows, width), F32),
        scratch_shapes=[pltpu.VMEM((tokens, width), BF)],
        compiler_params=pltpu.CompilerParams(vmem_limit_bytes=40 << 20),
        cost_estimate=pl.CostEstimate(
            flops=2 * rows * (2 * tokens + slots) * width, bytes_accessed=16 << 20, transcendentals=0
        ),
    )(p_own, p_sib, *hidden, h_sib, extra, at)


def ranks(inside):
    n = inside.shape[-1]
    before = jnp.arange(n)[:, None] < jnp.arange(n)[None, :]
    return jnp.einsum(
        "...j,jk->...k", inside.astype(BF), before.astype(BF), preferred_element_type=F32
    ).astype(jnp.int32)


def pick(slot_of, inside, first_slot):
    slots = first_slot + jnp.arange(SLOTS, dtype=jnp.int32)
    return (slot_of[..., None, :] == slots[:, None]) & inside[..., None, :]


def per_device(hidden_states, tied_table, labels, dec_ids, enc_ids, dec_grad, enc_grad):
    row_count, model_width = tied_table.shape
    v, t = lax.axis_index("vocab"), lax.axis_index("tok")
    y, core = t // 2, t % 2
    own_first = (v * 8 + t) * row_count
    sib_first = (v * 8 + (t ^ 1)) * row_count
    chip_rows = 2 * row_count
    chip_first = (v * 4 + y) * chip_rows

    hidden = [hidden_states] + [along_y(hidden_states, h) for h in HOPS[1:]]
    sib_table = sibling(tied_table)

    own_ids = jnp.concatenate([labels[None], dec_ids[None], enc_ids[None], jnp.zeros((5, 128), jnp.int32)])
    ids = jnp.stack([own_ids] + [along_y(own_ids, h) for h in HOPS[1:]])
    ids8 = jnp.concatenate([ids, sibling(ids)])

    lab8 = ids8[:, 0]
    lab_chip = lab8 // chip_rows
    same = lab8[:, :, None] == lab8[:, None, :]
    earlier = jnp.arange(128)[:, None] < jnp.arange(128)[None, :]
    is_first = ~jnp.any(same & earlier[None], axis=1)
    same_chip = lab_chip[:, :, None] == lab_chip[:, None, :]
    first_rank = jnp.sum((same_chip & earlier[None] & is_first[:, :, None]).astype(jnp.int32), axis=1)
    lab_rank = jnp.sum(jnp.where(same & is_first[:, :, None], first_rank[:, :, None], 0), axis=1)
    tok8 = jnp.concatenate([ids8[:, 1], ids8[:, 2]], axis=1)
    tok_chip = tok8 // chip_rows
    tok_inside = tok_chip == v * 4 + y
    tok_rank = ranks(tok_inside)
    all_chips = jnp.arange(64, dtype=jnp.int32)
    tok_most = jnp.max(jnp.sum((tok_chip[:, :, None] == all_chips).astype(jnp.int32), axis=1))
    lab_most = jnp.max(lab_rank) + 1
    lab_rounds = (lab_most + SLOTS - 1) // SLOTS
    tok_rounds = (tok_most + SLOTS - 1) // SLOTS

    own_tok = tok8[0]
    hop_y = jnp.stack([(y + h) % 4 for h in HOPS])
    send_inside = own_tok[None] // chip_rows == (v * 4 + hop_y)[:, None]
    send_rank = ranks(send_inside)
    own_grads = jnp.concatenate([dec_grad, enc_grad])

    def token_rows(first_slot):
        chosen = pick(send_rank, send_inside, first_slot).reshape(4 * SLOTS, 256)
        return jnp.dot(chosen.astype(BF), own_grads, preferred_element_type=F32).astype(BF)

    def token_places(first_slot):
        chosen = pick(tok_rank, tok_inside, first_slot)
        at = jnp.sum(jnp.where(chosen, (tok8 - own_first + row_count * 4)[:, None, :], 0), axis=2)
        return (jnp.where(at == 0, -(1 << 20), at) - row_count * 4).reshape(1, 8 * SLOTS)

    def label_rows(first_slot):
        chosen = pick(lab_rank[:4], (lab_chip[:4] == v * 4 + y) & is_first[:4], first_slot)
        at = jnp.sum(jnp.where(chosen, (lab8[:4] - chip_first + 1)[:, None, :], 0), axis=2) - 1
        at = at.reshape(4 * SLOTS)
        at = jnp.where(at < 0, -(1 << 20), at) + chip_first
        row = jnp.arange(row_count, dtype=jnp.int32)
        from_own = ((at - own_first)[:, None] == row).astype(BF)
        from_sib = ((at - sib_first)[:, None] == row).astype(BF)
        got = jnp.dot(from_own, tied_table, preferred_element_type=F32)
        return (got + jnp.dot(from_sib, sib_table, preferred_element_type=F32)).astype(BF)

    def label_place(rows, first_slot):
        slot = jnp.arange(4 * SLOTS, dtype=jnp.int32)
        source = jnp.repeat(v * 4 + hop_y, SLOTS)
        to = (lab_chip[0][:, None] == source[None]) & (
            lab_rank[0][:, None] == (slot % SLOTS + first_slot)[None]
        )
        return jnp.dot(to.astype(BF), rows, preferred_element_type=F32).astype(BF)

    def exchange(rows):
        return [rows[0]] + [along_y(rows[i], -HOPS[i]) for i in (2, 1, 3)]

    to_send = jnp.concatenate(
        [label_rows(0).reshape(4, SLOTS, -1), token_rows(0).reshape(4, SLOTS, -1)], axis=1
    )
    received = jnp.stack(exchange([to_send[i] for i in range(4)]))
    label_state = label_place(received[:, :SLOTS].reshape(4 * SLOTS, -1), 0)
    tok_received = received[:, SLOTS:].reshape(4 * SLOTS, -1)
    tok_received = jnp.concatenate([tok_received, sibling(tok_received)])

    def more_labels(carry):
        r, state = carry
        rows = label_rows(r * SLOTS).reshape(4, SLOTS, -1)
        got = jnp.concatenate(exchange([rows[i] for i in range(4)]))
        return r + 1, state + label_place(got, r * SLOTS)

    _, label_state = lax.while_loop(lambda c: c[0] < lab_rounds, more_labels, (jnp.int32(1), label_state))

    lab4 = ids[:, 0].reshape(512)
    lab_rel = jnp.stack([lab4 - own_first, lab4 - sib_first], axis=1)
    logits_a, stats_a, grad0, grad1, grad2 = logits_and_grads(hidden[:3], tied_table, sib_table, lab_rel[:384])
    logits_b, stats_b, grad3 = logits_and_grads(hidden[3:], tied_table, sib_table, lab_rel[384:])

    grads = exchange([grad0, grad1, grad2, grad3])

    relative = jnp.concatenate([stats_a, stats_b], axis=1).reshape(8, 4, 128)
    canonical = jnp.stack(
        [
            sum(jnp.where(hop_y[h] == i, relative[:, h], 0.0) for h in range(4))
            for i in range(4)
        ],
        axis=1,
    ).reshape(8, 512)

    def merge(parts):
        peaks = functools.reduce(jnp.maximum, [p[0] for p in parts])
        total = sum(p[1] * jnp.exp(p[0] - peaks) for p in parts)
        return jnp.concatenate(
            [peaks[None], total[None], sum(p[2] for p in parts)[None], jnp.zeros((5, 512), F32)]
        )

    from_y = [canonical] + [along_y(canonical, h) for h in HOPS[1:]]
    stats = merge(from_y)
    stats = merge([stats] + [along_z(stats, h) for h in HOPS[1:]])
    stats = merge([stats] + [along_x(stats, h) for h in HOPS[1:]])
    log_norm, picked = stats[0] + jnp.log(stats[1]), stats[2]

    def mine(x):
        return lax.dynamic_slice_in_dim(x, y * 128, 128)

    my_norm, my_picked = mine(log_norm), mine(picked)
    token_loss = my_norm - my_picked

    scales = jnp.stack([jnp.exp(mine(s[0]) - my_norm) for s in from_y] + [jnp.exp(my_picked - my_norm) - 1.0])
    group_sum = scales[4][:, None] * label_state.astype(F32)
    for i in range(4):
        group_sum = group_sum + scales[i][:, None] * grads[i].astype(F32)
    parts = group_sum.reshape(128, 16, model_width // 16).transpose(1, 0, 2)
    grad_hidden = jnp.sum(lax.all_to_all(parts, "vocab", 0, 0), axis=0)

    norm_rel = jnp.concatenate(
        [lax.dynamic_slice_in_dim(log_norm, hop_y[h] * 128, 128) for h in range(4)]
    )

    def logit_grad(first_chunk, first_row):
        column = jnp.arange(row_count, dtype=jnp.int32) + first_row
        blocks = []
        for logits, lo, hi in ((logits_a, 0, 384), (logits_b, 384, 512)):
            part = logits[first_chunk : first_chunk + 2].transpose(1, 0, 2).reshape(hi - lo, row_count)
            is_label = lab4[lo:hi, None] == column[None]
            blocks.append((jnp.exp(part - norm_rel[lo:hi, None]) - is_label.astype(F32)).astype(BF))
        return jnp.concatenate(blocks)

    p_own = logit_grad(0, own_first)
    p_sib = sibling(logit_grad(2, sib_first))
    hidden_sib = sibling(jnp.concatenate(hidden))
    grad_table = table_gradient(p_own, p_sib, hidden, hidden_sib, tok_received, token_places(0))

    def more_tokens(carry):
        r, grad = carry
        rows = token_rows(r * SLOTS).reshape(4, SLOTS, -1)
        got = jnp.concatenate(exchange([rows[i] for i in range(4)]))
        got = jnp.concatenate([got, sibling(got)])
        named = token_places(r * SLOTS) == jnp.arange(row_count, dtype=jnp.int32)[:, None]
        return r + 1, grad + jnp.dot(named.astype(BF), got, preferred_element_type=F32)

    _, grad_table = lax.while_loop(lambda c: c[0] < tok_rounds, more_tokens, (jnp.int32(1), grad_table))
    return grad_table, grad_hidden, token_loss


def solution(mesh):
    in_specs = (
        P("tok", None),
        P(("vocab", "tok"), None),
        P("tok"),
        P("tok"),
        P("tok"),
        P("tok", None),
        P("tok", None),
    )
    out_specs = (P(("vocab", "tok"), None), P("tok", "vocab"), P("tok"))
    return jax.shard_map(
        per_device, mesh=mesh, in_specs=in_specs, out_specs=out_specs, check_vma=False
    )
```

```python
import functools

import jax
import jax.numpy as jnp
from jax import lax
from jax.experimental import pallas as pl
from jax.experimental.pallas import tpu as pltpu
from jax.sharding import PartitionSpec as P

BF = jnp.bfloat16
F32 = jnp.float32
I32 = jnp.int32
SLOTS = 16
HOPS = (0, 1, 3, 2)
BACK = (0, 2, 1, 3)
BLOCK = 128
HALF = 1024
CHUNK = 512
NEAR = 4 * BLOCK
PAYLOAD = BLOCK + 2 * SLOTS


def along_y(x, hop):
    pairs = [(t, ((t // 2 - hop) % 4) * 2 + t % 2) for t in range(8)]
    return lax.ppermute(x, "tok", pairs)


def partner(place, step):
    return 3 - place if step else place ^ 1


def swap_z(x, step):
    return lax.ppermute(x, "vocab", [(v, v // 4 * 4 + partner(v % 4, step)) for v in range(16)])


def swap_x(x, step):
    return lax.ppermute(x, "vocab", [(v, partner(v // 4, step) * 4 + v % 4) for v in range(16)])


def swap_y(x, step):
    return lax.ppermute(x, "tok", [(t, partner(t // 2, step) * 2 + t % 2) for t in range(8)])


def sibling(x):
    return lax.ppermute(x, "tok", [(t, t ^ 1) for t in range(8)])


def place():
    t = lax.axis_index("tok")
    return lax.axis_index("vocab"), t // 2, t % 2


def one(mask):
    return jnp.where(mask, 1.0, 0.0)


def iota(shape, dim):
    return lax.broadcasted_iota(I32, shape, dim)


def transposed(rows):
    return jnp.concatenate([rows, jnp.zeros((120, rows.shape[1]), F32)], axis=0).T


def whole(*shape):
    return pl.BlockSpec(shape, lambda *_: (0,) * len(shape), pipeline_mode=pl.Buffered(1))


VMEM = pl.BlockSpec(memory_space=pltpu.VMEM)


def params(limit=60 << 20):
    return pltpu.CompilerParams(vmem_limit_bytes=limit)


SMALL = 12 << 20


def cost(us):
    return pl.CostEstimate(flops=int(us * 1e9), bytes_accessed=1024, transcendentals=0)


def rows_kernel(label_ref, dec_id_ref, enc_id_ref, dec_ref, enc_ref, rows_ref, ids_out):
    v, y, _ = place()
    ids = jnp.concatenate(
        [label_ref[...], dec_id_ref[...], enc_id_ref[...], jnp.zeros((5, BLOCK), I32)], axis=0
    )
    ids_out[...] = ids
    chip = lax.shift_right_logical(ids, 11)
    inside = []
    for kind in (1, 2):
        inside += [one(chip[kind : kind + 1] == v * 4 + lax.rem(y + h, 4)) for h in HOPS]
        inside += [jnp.zeros((4, BLOCK), F32)]
    inside = jnp.concatenate(inside, axis=0)
    before = one(iota((BLOCK, BLOCK), 0) < iota((BLOCK, BLOCK), 1)).astype(BF)
    rank = jnp.dot(inside.astype(BF), before, preferred_element_type=F32)
    rank_enc = rank[8:16] + jnp.sum(inside[0:8], axis=1, keepdims=True)
    slot = iota((SLOTS, BLOCK), 0).astype(F32)

    def chosen(rank, inside):
        return jnp.concatenate(
            [one(rank[i : i + 1] == slot) * inside[i : i + 1] for i in range(4)], axis=0
        ).astype(BF)

    got = jnp.dot(chosen(rank[0:8], inside[0:8]), dec_ref[...], preferred_element_type=F32)
    got += jnp.dot(chosen(rank_enc, inside[8:16]), enc_ref[...], preferred_element_type=F32)
    rows_ref[...] = got.astype(BF)


def rows_to_send(labels, dec_ids, enc_ids, dec_grad, enc_grad):
    width = dec_grad.shape[1]
    return pl.pallas_call(
        rows_kernel,
        in_specs=[VMEM] * 5,
        out_specs=[VMEM] * 2,
        out_shape=[jax.ShapeDtypeStruct((4 * SLOTS, width), BF), jax.ShapeDtypeStruct((8, BLOCK), I32)],
        compiler_params=params(),
        cost_estimate=cost(1000),
    )(labels[None], dec_ids[None], enc_ids[None], dec_grad, enc_grad)


def plan_kernel(p0, p1, p2, p3, label_col, slot_col, place_col, pick_ref, most_ref):
    v, y, core = place()
    my_chip = v * 4 + y
    pairs = (p0, p1, p2, p3)

    def kind(k):
        return jnp.concatenate(
            [pairs[i][8 * c + k : 8 * c + k + 1, :] for c in range(2) for i in range(4)], axis=0
        )

    lab, dec, enc = kind(0), kind(1), kind(2)

    def relative(ids):
        return ((ids - my_chip * (2 * HALF)) ^ (core * HALF)).astype(F32)

    def chip_of(ids):
        return lax.shift_right_logical(ids, 11).astype(F32)

    mine = my_chip.astype(F32)
    lab_f, lab_rel, lab_chip = lab.astype(F32), relative(lab), chip_of(lab)
    lab_t, rel_t, chip_t = transposed(lab_f), transposed(lab_rel), transposed(lab_chip)
    earlier = one(iota((BLOCK, BLOCK), 0) < iota((BLOCK, BLOCK), 1))
    later = one(iota((BLOCK, BLOCK), 0) > iota((BLOCK, BLOCK), 1))
    slot = iota((SLOTS, BLOCK), 0).astype(F32)
    most = jnp.zeros((1, 1), F32)
    for b in range(8):
        same = one(lab_t[:, b : b + 1] == lab_f[b : b + 1, :])
        same_chip = one(chip_t[:, b : b + 1] == lab_chip[b : b + 1, :])
        first_row = one(jnp.sum(same * earlier, axis=0, keepdims=True) == 0.0)
        first_col = one(jnp.sum(same * later, axis=1, keepdims=True) == 0.0)
        rank = jnp.sum(same_chip * earlier * first_col, axis=0, keepdims=True)
        most = jnp.maximum(most, jnp.max(rank * first_row, axis=1, keepdims=True) + 1.0)
        label_col[BLOCK * b : BLOCK * (b + 1), :] = rel_t[:, b : b + 1].astype(I32)
        if b < 4:
            chosen = one(rank == slot) * (first_row * one(lab_chip[b : b + 1] == mine))
            at = jnp.sum(chosen * (lab_rel[b : b + 1] + 1.0), axis=1, keepdims=True) - 1.0
            slot_col[SLOTS * b : SLOTS * (b + 1), :] = at.astype(I32)
        if b == 0:
            rank_col = jnp.sum(same * (first_row * rank), axis=1, keepdims=True)
            lane = iota((BLOCK, BLOCK), 1)
            source = lane // SLOTS
            hop = jnp.where(source == 2, 3, jnp.where(source == 3, 2, source))
            chip = (v * 4 + lax.rem(y + hop, 4)).astype(F32)
            hit = one(chip_t[:, 0:1] == chip) * one(rank_col == (lane % SLOTS).astype(F32))
            pick_ref[...] = (hit * one(lane < 4 * SLOTS)).astype(BF)

    dec_chip, enc_chip = chip_of(dec), chip_of(enc)
    dec_rel, enc_rel = relative(dec), relative(enc)
    inside = jnp.concatenate([one(dec_chip == mine), one(enc_chip == mine)], axis=0)
    rank = jnp.dot(inside.astype(BF), earlier.astype(BF), preferred_element_type=F32)
    rank_enc = rank[8:16] + jnp.sum(inside[0:8], axis=1, keepdims=True)
    all_chips = iota((64, BLOCK), 0).astype(F32)
    tok_most = jnp.zeros((1, 1), F32)
    for b in range(8):
        row = slice(b, b + 1)
        at = one(rank[row] == slot) * inside[row] * (dec_rel[row] + 1.0)
        at += one(rank_enc[row] == slot) * inside[8 + b : 9 + b] * (enc_rel[row] + 1.0)
        at = jnp.sum(at, axis=1, keepdims=True) - 1.0
        place_col[SLOTS * b : SLOTS * (b + 1), :] = at.astype(I32)
        count = one(dec_chip[row] == all_chips) + one(enc_chip[row] == all_chips)
        count = jnp.sum(count, axis=1, keepdims=True)
        tok_most = jnp.maximum(tok_most, jnp.max(count, axis=0, keepdims=True))
    most_ref[...] = jnp.where(iota((8, BLOCK), 1) == 0, most, tok_most).astype(I32)


def plan(pairs):
    return pl.pallas_call(
        plan_kernel,
        in_specs=[VMEM] * 4,
        out_specs=[VMEM] * 5,
        out_shape=[
            jax.ShapeDtypeStruct((8 * BLOCK, 1), I32),
            jax.ShapeDtypeStruct((4 * SLOTS, 1), I32),
            jax.ShapeDtypeStruct((8 * SLOTS, 1), I32),
            jax.ShapeDtypeStruct((BLOCK, BLOCK), BF),
            jax.ShapeDtypeStruct((8, BLOCK), I32),
        ],
        compiler_params=params(),
        cost_estimate=cost(100),
    )(*pairs)


def logits_kernel(*refs):
    hidden = refs[:4]
    own_ref, sib_ref, label_ref, slot_ref, rows_ref = refs[4:9]
    own_out, sib_out, stats_ref = refs[9:12]
    payload = refs[12:16]
    states, table, logits, weights, in_sem, hidden_sem, out_sem = refs[16:]
    blocks = []
    for i in range(4):
        blocks.append(
            pltpu.make_async_copy(hidden[i], states.at[pl.ds(BLOCK * i, BLOCK)], hidden_sem.at[i])
        )
        blocks[i].start()
    loads = []
    for j in range(4):
        source = own_ref if j < 2 else sib_ref
        loads.append(
            pltpu.make_async_copy(
                source.at[pl.ds(CHUNK * (j % 2), CHUNK)], table.at[pl.ds(CHUNK * j, CHUNK)], in_sem.at[j]
            )
        )
        loads[j].start()
    for i in range(4):
        payload[i][BLOCK + SLOTS : PAYLOAD, :] = rows_ref[SLOTS * i : SLOTS * (i + 1), :]
    for block in blocks:
        block.wait()

    label = label_ref[0:NEAR, :]
    stores = []
    peak = None
    for j in range(4):
        loads[j].wait()
        part = lax.dot_general(
            states[...], table[CHUNK * j : CHUNK * (j + 1), :], (((1,), (1,)), ((), ())), preferred_element_type=F32
        )
        logits[j] = part
        target = own_out if j < 2 else sib_out
        stores.append(pltpu.make_async_copy(logits.at[j], target.at[j % 2], out_sem.at[j]))
        stores[j].start()
        top = jnp.max(part, axis=1, keepdims=True)
        peak = top if peak is None else jnp.maximum(peak, top)

    total = picked = None
    for j in range(4):
        part = logits[j]
        is_label = iota((NEAR, CHUNK), 1) + CHUNK * j == label
        weight = jnp.exp(part - peak)
        row_sum = jnp.sum(weight, axis=1, keepdims=True)
        hit = jnp.sum(jnp.where(is_label, part, 0.0), axis=1, keepdims=True)
        total = row_sum if total is None else total + row_sum
        picked = hit if picked is None else picked + hit
        at = slice(CHUNK * j, CHUNK * (j + 1))
        weights[0:NEAR, at] = jnp.where(is_label, 0.0, weight).astype(BF)
        slots = iota((4 * SLOTS, CHUNK), 1) + CHUNK * j == slot_ref[...]
        weights[NEAR:, at] = one(slots).astype(BF)

    lane = iota((NEAR, 128), 1)
    both = jnp.where(lane == 0, peak, jnp.where(lane == 1, total, jnp.where(lane == 2, picked, 0.0)))
    stats_ref[...] = both.T[0:8, :]
    for j in range(4):
        at = slice(CHUNK * j, CHUNK * (j + 1))
        grad = jnp.dot(weights[...], table[:, at], preferred_element_type=F32).astype(BF)
        for i in range(4):
            payload[i][0:BLOCK, at] = grad[BLOCK * i : BLOCK * (i + 1)]
            payload[i][BLOCK : BLOCK + SLOTS, at] = grad[NEAR + SLOTS * i : NEAR + SLOTS * (i + 1)]
    for store in stores:
        store.wait()


def logits_and_grads(hidden, own, sib, labels, slots, rows):
    width = own.shape[1]
    anywhere = pl.BlockSpec(memory_space=pl.ANY)
    return pl.pallas_call(
        logits_kernel,
        in_specs=[anywhere] * 6 + [VMEM] * 3,
        out_specs=[anywhere] * 2 + [VMEM] * 5,
        out_shape=[jax.ShapeDtypeStruct((2, NEAR, CHUNK), F32)] * 2
        + [jax.ShapeDtypeStruct((8, NEAR), F32)]
        + [jax.ShapeDtypeStruct((PAYLOAD, width), BF)] * 4,
        scratch_shapes=[
            pltpu.VMEM((NEAR, width), BF),
            pltpu.VMEM((2 * HALF, width), BF),
            pltpu.VMEM((4, NEAR, CHUNK), F32),
            pltpu.VMEM((NEAR + 4 * SLOTS, 2 * HALF), BF),
            pltpu.SemaphoreType.DMA((4,)),
            pltpu.SemaphoreType.DMA((4,)),
            pltpu.SemaphoreType.DMA((4,)),
        ],
        compiler_params=params(),
        cost_estimate=cost(12),
    )(*hidden, own, sib, labels, slots, rows)


def merged(parts):
    top = functools.reduce(jnp.maximum, [p[0:1] for p in parts])
    total = sum(p[1:2] * jnp.exp(p[0:1] - top) for p in parts)
    return top, total, sum(p[2:3] for p in parts)


def small(kernel, out_shape, *operands, scratch=()):
    many = isinstance(out_shape, list)
    return pl.pallas_call(
        kernel,
        in_specs=[VMEM] * len(operands),
        out_specs=[VMEM] * len(out_shape) if many else VMEM,
        out_shape=out_shape,
        scratch_shapes=scratch,
        compiler_params=params(SMALL),
    )(*operands)


def order_kernel(stats_ref, out_ref):
    _, y, _ = place()
    stats = stats_ref[...]
    rows = jnp.concatenate([stats[0:3], stats[0:1], jnp.zeros((4, NEAR), F32)], axis=0)
    for i in range(4):
        at = pl.multiple_of(lax.rem(y + HOPS[i], 4) * BLOCK, BLOCK)
        out_ref[:, pl.ds(at, BLOCK)] = rows[:, BLOCK * i : BLOCK * (i + 1)]


def merge_kernel(own_ref, other_ref, out_ref):
    own = own_ref[...]
    out_ref[...] = jnp.concatenate([*merged([own, other_ref[...]]), own[3:8]], axis=0)


def merge_y_kernel(own_ref, other_ref, out_ref):
    _, y, _ = place()
    own, other = own_ref[...], other_ref[...]
    odd = lax.rem(y, 2) == 1
    even_peaks = jnp.where(odd, other[3:4], own[3:4])
    odd_peaks = jnp.where(odd, own[3:4], other[3:4])
    out_ref[...] = jnp.concatenate(
        [*merged([own, other]), even_peaks, odd_peaks, jnp.zeros((3, NEAR), F32)], axis=0
    )


def norm_kernel(own_ref, other_ref, row_ref, col_ref, loss_ref, all_ref):
    _, y, _ = place()
    own, other = own_ref[...], other_ref[...]
    top, total, picked = merged([own, other])
    norm = top + jnp.log(total)
    low = jnp.where(y < 2, own[3:5], other[3:5])
    high = jnp.where(y < 2, other[3:5], own[3:5])
    all_ref[...] = jnp.concatenate([norm, picked, low, high, jnp.zeros((2, NEAR), F32)], axis=0)

    def block(i):
        return all_ref[:, pl.ds(pl.multiple_of(lax.rem(y + HOPS[i], 4) * BLOCK, BLOCK), BLOCK)]

    mine = block(0)
    scales = []
    for i in range(4):
        source = lax.rem(y + HOPS[i], 4)
        peaks = sum(jnp.where(source == k, mine[2 + k : 3 + k], 0.0) for k in range(4))
        scales.append(jnp.exp(peaks - mine[0:1]))
    label = jnp.exp(mine[1:2] - mine[0:1]) - 1.0
    row_ref[...] = jnp.concatenate([*scales, label, jnp.zeros((3, BLOCK), F32)], axis=0)
    loss_ref[...] = mine[0:1] - mine[1:2]
    col_ref[...] = transposed(jnp.concatenate([block(i) for i in range(4)], axis=1))[:, 0:1]


def norms(stats):
    shape = jax.ShapeDtypeStruct((8, NEAR), F32)
    sums = small(order_kernel, shape, stats)
    for swap in (swap_z, swap_x):
        for step in range(2):
            sums = small(merge_kernel, shape, sums, swap(sums, step))
    sums = small(merge_y_kernel, shape, sums, swap_y(sums, 0))
    return small(
        norm_kernel,
        [
            jax.ShapeDtypeStruct((8, BLOCK), F32),
            jax.ShapeDtypeStruct((NEAR, 1), F32),
            jax.ShapeDtypeStruct((1, BLOCK), F32),
        ],
        sums,
        swap_y(sums, 1),
        scratch=[pltpu.VMEM((8, NEAR), F32)],
    )


def combine_kernel(p0, p1, p2, p3, scale_ref, pick_ref, late_ref, parts_ref, rows_ref):
    payload = (p0, p1, p2, p3)
    cols = transposed(scale_ref[...])
    for i in range(4):
        rows_ref[SLOTS * i : SLOTS * (i + 1), :] = payload[i][BLOCK + SLOTS : PAYLOAD, :]
    slots = jnp.concatenate([p[BLOCK : BLOCK + SLOTS, :] for p in payload], axis=0)
    label_rows = jnp.dot(pick_ref[:, 0 : 4 * SLOTS], slots, preferred_element_type=F32)
    total = cols[:, 4:5] * (label_rows + late_ref[...].astype(F32))
    for i in range(4):
        total += cols[:, i : i + 1] * payload[i][0:BLOCK, :].astype(F32)
    for i in range(parts_ref.shape[0]):
        parts_ref[i] = total[:, 128 * i : 128 * (i + 1)]


def sum_kernel(groups_ref, end_ref, out_ref):
    out_ref[...] = jnp.sum(groups_ref[...], axis=0) + end_ref[0:1, :]


def combine(payload, scales, pick, late_rows):
    width = payload[0].shape[1]
    return pl.pallas_call(
        combine_kernel,
        in_specs=[VMEM] * 7,
        out_specs=[VMEM] * 2,
        out_shape=[
            jax.ShapeDtypeStruct((16, BLOCK, width // 16), F32),
            jax.ShapeDtypeStruct((4 * SLOTS, width), BF),
        ],
        compiler_params=params(16 << 20),
        cost_estimate=cost(0.001),
    )(*payload, scales, pick, late_rows)


def table_kernel(*refs):
    logits = refs[0:2]
    norms_of = refs[2:4]
    label_ref, place_ref = refs[4:6]
    hidden = refs[6:14]
    rows_own, rows_sib, out_ref, end_ref, states, grads = refs[14:]
    tokens = NEAR

    @pl.when(pl.program_id(0) == 0)
    def _():
        for i in range(8):
            states[BLOCK * i : BLOCK * (i + 1), :] = hidden[i][...]
        states[2 * tokens : 2 * tokens + 4 * SLOTS, :] = rows_own[...]
        states[2 * tokens + 4 * SLOTS :, :] = rows_sib[...]

    tile = out_ref.shape[0]
    first = pl.program_id(0) * tile
    for k in range(2):
        low = tokens * k
        value = jnp.exp(logits[k][0] - norms_of[k][...])
        is_label = iota((tokens, tile), 1) + first == label_ref[low : low + tokens, :]
        grads[low : low + tokens, :] = (value - one(is_label)).astype(BF)
    named = iota((8 * SLOTS, tile), 1) + first == place_ref[...]
    grads[2 * tokens :, :] = one(named).astype(BF)
    end_ref[...] = jnp.zeros_like(end_ref)
    out_ref[...] = lax.dot_general(
        grads[...], states[...], (((0,), (0,)), ((), ())), preferred_element_type=F32
    )


def table_gradient(logits, norm_own, norm_sib, labels, places, hidden, rows_own, rows_sib):
    width, tile, tokens = hidden[0].shape[1], 256, NEAR
    per = CHUNK // tile
    return pl.pallas_call(
        table_kernel,
        grid=(HALF // tile,),
        in_specs=[pl.BlockSpec((1, l.shape[1], tile), lambda j: (j // per, 0, j % per)) for l in logits]
        + [whole(tokens, 1), whole(tokens, 1), whole(2 * tokens, 1), whole(8 * SLOTS, 1)]
        + [whole(BLOCK, width)] * 8
        + [whole(4 * SLOTS, width)] * 2,
        out_specs=[pl.BlockSpec((tile, width), lambda j: (j, 0)), pl.BlockSpec((8, 128), lambda j: (0, 0))],
        out_shape=[jax.ShapeDtypeStruct((HALF, width), F32), jax.ShapeDtypeStruct((8, 128), F32)],
        scratch_shapes=[
            pltpu.VMEM((2 * tokens + 8 * SLOTS, width), BF),
            pltpu.VMEM((2 * tokens + 8 * SLOTS, tile), BF),
        ],
        compiler_params=params(),
        cost_estimate=pl.CostEstimate(
            flops=2 * HALF * (2 * tokens + 8 * SLOTS) * width, bytes_accessed=16 << 20, transcendentals=0
        ),
    )(*logits, norm_own, norm_sib, labels, places, *hidden, rows_own, rows_sib)


def ranks(inside):
    n = inside.shape[-1]
    before = jnp.arange(n)[:, None] < jnp.arange(n)[None, :]
    return jnp.sum((inside[..., :, None] & before).astype(I32), axis=-2)


def pick(slot_of, inside, first_slot):
    slots = first_slot + jnp.arange(SLOTS, dtype=I32)
    return (slot_of[..., None, :] == slots[:, None]) & inside[..., None, :]


def exchange(rows):
    return [rows[0]] + [along_y(rows[BACK[i]], HOPS[i]) for i in range(1, 4)]


def more_label_rows(pairs, own_table, sib_table, first_slot):
    v, y, core = place()
    labels = jnp.stack([p[0] for p in pairs])
    chip = labels // (2 * HALF)
    same = labels[:, :, None] == labels[:, None, :]
    earlier = jnp.arange(BLOCK)[:, None] < jnp.arange(BLOCK)[None, :]
    is_first = ~jnp.any(same & earlier, axis=1)
    same_chip = chip[:, :, None] == chip[:, None, :]
    first_rank = jnp.sum((same_chip & earlier & is_first[:, :, None]).astype(I32), axis=1)
    rank = jnp.sum(jnp.where(same & is_first[:, :, None], first_rank[:, :, None], 0), axis=1)
    relative = (labels - (v * 4 + y) * (2 * HALF)) ^ (core * HALF)
    chosen = pick(rank, (chip == v * 4 + y) & is_first, first_slot)
    at = (jnp.sum(jnp.where(chosen, relative[:, None, :] + 1, 0), axis=2) - 1).reshape(4 * SLOTS, 1)
    row = jnp.arange(HALF, dtype=I32)
    rows = jnp.dot((at == row).astype(BF), own_table, preferred_element_type=F32)
    rows += jnp.dot((at == row + HALF).astype(BF), sib_table, preferred_element_type=F32)
    rows = rows.astype(BF).reshape(4, SLOTS, -1)
    got = jnp.concatenate(exchange([rows[i] for i in range(4)]))
    slot = jnp.arange(4 * SLOTS, dtype=I32)
    source = jnp.stack([v * 4 + (y + h) % 4 for h in HOPS])[slot // SLOTS]
    hit = (chip[0][:, None] == source[None]) & (rank[0][:, None] == (slot % SLOTS + first_slot)[None])
    return jnp.dot(hit.astype(BF), got, preferred_element_type=F32)


def more_token_rows(pairs, dec_grad, enc_grad, first_slot):
    v, y, core = place()
    own = jnp.concatenate([pairs[0][1], pairs[0][2]])
    chips = jnp.stack([v * 4 + (y + h) % 4 for h in HOPS])
    inside = own[None] // (2 * HALF) == chips[:, None]
    chosen = pick(ranks(inside), inside, first_slot).reshape(4 * SLOTS, 2 * BLOCK)
    rows = jnp.dot(chosen.astype(BF), jnp.concatenate([dec_grad, enc_grad]), preferred_element_type=F32)
    rows = rows.astype(BF).reshape(4, SLOTS, -1)
    got = jnp.concatenate(exchange([rows[i] for i in range(4)]))
    got = jnp.concatenate([got, sibling(got)])
    ids = jnp.stack(
        [jnp.concatenate([p[8 * c + 1], p[8 * c + 2]]) for c in range(2) for p in pairs]
    )
    inside = ids // (2 * HALF) == v * 4 + y
    chosen = pick(ranks(inside), inside, first_slot)
    relative = (ids - (v * 4 + y) * (2 * HALF)) ^ (core * HALF)
    at = jnp.sum(jnp.where(chosen, relative[:, None, :] + 1, 0), axis=2).reshape(1, 8 * SLOTS) - 1
    named = at == jnp.arange(HALF, dtype=I32)[:, None]
    return jnp.dot(named.astype(BF), got, preferred_element_type=F32)


def per_device(hidden_states, tied_table, labels, dec_ids, enc_ids, dec_grad, enc_grad):
    after, before = along_y(hidden_states, 1), along_y(hidden_states, -1)
    sib_table = sibling(tied_table)
    rows, ids = rows_to_send(labels, dec_ids, enc_ids, dec_grad, enc_grad)
    own_pair = jnp.concatenate([ids, sibling(ids)])
    pairs = [own_pair] + [along_y(own_pair, h) for h in HOPS[1:]]
    far = jnp.concatenate([along_y(after[:64], 1), along_y(before[64:], -1)])
    hidden = [hidden_states, after, before, far]
    label_col, slot_col, place_col, label_pick, most = plan(pairs)
    label_rounds = (most[0, 0] + SLOTS - 1) // SLOTS
    token_rounds = (most[0, 1] + SLOTS - 1) // SLOTS

    own_logits, sib_logits, stats, *payload = logits_and_grads(
        hidden, tied_table, sib_table, label_col, slot_col, rows
    )

    payload = exchange(payload)
    scales, norm_col, loss = norms(stats)

    def add_labels(carry):
        r, state = carry
        pairs_r, slot = lax.optimization_barrier((pairs, r * SLOTS))
        return r + 1, state + more_label_rows(pairs_r, tied_table, sib_table, slot).astype(BF)

    none = jnp.zeros((BLOCK, tied_table.shape[1]), BF)
    _, late_rows = lax.while_loop(lambda c: c[0] < label_rounds, add_labels, (jnp.int32(1), none))
    group, rows_own = combine(payload, scales, label_pick, late_rows)
    groups_of = lax.all_to_all(group, "vocab", 0, 0)

    grad_table, end = table_gradient(
        [own_logits, sibling(sib_logits)],
        norm_col,
        sibling(norm_col),
        label_col,
        place_col,
        hidden + [sibling(h) for h in hidden],
        rows_own,
        sibling(rows_own),
    )

    grad_hidden = small(
        sum_kernel, jax.ShapeDtypeStruct(groups_of.shape[1:], F32), groups_of, end
    )

    def add_tokens(carry):
        r, grad = carry
        pairs_r, dec, enc, slot = lax.optimization_barrier((pairs, dec_grad, enc_grad, r * SLOTS))
        return r + 1, grad + more_token_rows(pairs_r, dec, enc, slot)

    _, grad_table = lax.while_loop(lambda c: c[0] < token_rounds, add_tokens, (jnp.int32(1), grad_table))
    return grad_table, grad_hidden, loss.reshape(BLOCK)


def solution(mesh):
    in_specs = (
        P("tok", None),
        P(("vocab", "tok"), None),
        P("tok"),
        P("tok"),
        P("tok"),
        P("tok", None),
        P("tok", None),
    )
    out_specs = (P(("vocab", "tok"), None), P("tok", "vocab"), P("tok"))
    return jax.shard_map(
        per_device, mesh=mesh, in_specs=in_specs, out_specs=out_specs, check_vma=False
    )
```

```python
import functools

import jax
import jax.numpy as jnp
from jax import lax
from jax.experimental import pallas as pl
from jax.experimental.pallas import tpu as pltpu
from jax.sharding import PartitionSpec as P

BF = jnp.bfloat16
F32 = jnp.float32
I32 = jnp.int32
SLOTS = 16
HOPS = (0, 1, 3, 2)
BACK = (0, 2, 1, 3)
BLOCK = 128
HALF = 1024
CHUNK = 512
NEAR = 4 * BLOCK
PAYLOAD = BLOCK + 2 * SLOTS


def along_y(x, hop):
    pairs = [(t, ((t // 2 - hop) % 4) * 2 + t % 2) for t in range(8)]
    return lax.ppermute(x, "tok", pairs)


def partner(place, step):
    return 3 - place if step else place ^ 1


def swap_z(x, step):
    return lax.ppermute(x, "vocab", [(v, v // 4 * 4 + partner(v % 4, step)) for v in range(16)])


def swap_x(x, step):
    return lax.ppermute(x, "vocab", [(v, partner(v // 4, step) * 4 + v % 4) for v in range(16)])


def swap_y(x, step):
    return lax.ppermute(x, "tok", [(t, partner(t // 2, step) * 2 + t % 2) for t in range(8)])


def sibling(x):
    return lax.ppermute(x, "tok", [(t, t ^ 1) for t in range(8)])


def place():
    t = lax.axis_index("tok")
    return lax.axis_index("vocab"), t // 2, t % 2


def one(mask):
    return jnp.where(mask, 1.0, 0.0)


def iota(shape, dim):
    return lax.broadcasted_iota(I32, shape, dim)


def transposed(rows):
    return jnp.concatenate([rows, jnp.zeros((120, rows.shape[1]), F32)], axis=0).T


def whole(*shape):
    return pl.BlockSpec(shape, lambda *_: (0,) * len(shape), pipeline_mode=pl.Buffered(1))


VMEM = pl.BlockSpec(memory_space=pltpu.VMEM)


def params(limit=60 << 20):
    return pltpu.CompilerParams(vmem_limit_bytes=limit)


SMALL = 12 << 20


def cost(us):
    return pl.CostEstimate(flops=int(us * 1e9), bytes_accessed=1024, transcendentals=0)


def small(kernel, out_shape, *operands, scratch=()):
    many = isinstance(out_shape, list)
    return pl.pallas_call(
        kernel,
        in_specs=[VMEM] * len(operands),
        out_specs=[VMEM] * len(out_shape) if many else VMEM,
        out_shape=out_shape,
        scratch_shapes=scratch,
        compiler_params=params(SMALL),
    )(*operands)


def relay_kernel(after_ref, before_ref, i1, i2, i3, out_ref):
    _, _, core = place()
    out_ref[...] = jnp.where(core == 0, after_ref[...].astype(F32), before_ref[...].astype(F32)).astype(BF)


def farthest(after, before, ids):
    passed = small(relay_kernel, jax.ShapeDtypeStruct(after.shape, BF), after, before, *ids)
    return lax.ppermute(passed, "tok", [(t, (t + 2 if t % 2 else t - 2) % 8) for t in range(8)])


def rows_kernel(label_ref, dec_id_ref, enc_id_ref, dec_ref, enc_ref, rows_ref, ids_out):
    v, y, _ = place()
    ids = jnp.concatenate(
        [label_ref[...], dec_id_ref[...], enc_id_ref[...], jnp.zeros((5, BLOCK), I32)], axis=0
    )
    ids_out[...] = ids
    chip = lax.shift_right_logical(ids, 11)
    inside = []
    for kind in (1, 2):
        inside += [one(chip[kind : kind + 1] == v * 4 + lax.rem(y + h, 4)) for h in HOPS]
        inside += [jnp.zeros((4, BLOCK), F32)]
    inside = jnp.concatenate(inside, axis=0)
    before = one(iota((BLOCK, BLOCK), 0) < iota((BLOCK, BLOCK), 1)).astype(BF)
    rank = jnp.dot(inside.astype(BF), before, preferred_element_type=F32)
    rank_enc = rank[8:16] + jnp.sum(inside[0:8], axis=1, keepdims=True)
    slot = iota((SLOTS, BLOCK), 0).astype(F32)

    def chosen(rank, inside):
        return jnp.concatenate(
            [one(rank[i : i + 1] == slot) * one(slot < SLOTS - 1) * inside[i : i + 1] for i in range(4)], axis=0
        ).astype(BF)

    got = jnp.dot(chosen(rank[0:8], inside[0:8]), dec_ref[...], preferred_element_type=F32)
    got += jnp.dot(chosen(rank_enc, inside[8:16]), enc_ref[...], preferred_element_type=F32)
    rows_ref[...] = got.astype(BF)


def rows_to_send(labels, dec_ids, enc_ids, dec_grad, enc_grad):
    width = dec_grad.shape[1]
    return pl.pallas_call(
        rows_kernel,
        in_specs=[VMEM] * 5,
        out_specs=[VMEM] * 2,
        out_shape=[jax.ShapeDtypeStruct((4 * SLOTS, width), BF), jax.ShapeDtypeStruct((8, BLOCK), I32)],
        compiler_params=params(),
        cost_estimate=cost(1000),
    )(labels[None], dec_ids[None], enc_ids[None], dec_grad, enc_grad)


def plan_kernel(i0, i1, i2, i3, rows_ref):
    v, y, core = place()
    my_chip = v * 4 + y
    ids = (i0, i1, i2, i3)

    def kind(k):
        return jnp.concatenate([ids[i][k : k + 1, :] for i in range(4)] + [jnp.zeros((4, BLOCK), I32)], axis=0)

    lab, dec, enc = kind(0), kind(1), kind(2)

    def relative(ids):
        return ((ids - my_chip * (2 * HALF)) ^ (core * HALF)).astype(F32)

    def chip_of(ids):
        return lax.shift_right_logical(ids, 11).astype(F32)

    mine = my_chip.astype(F32)
    lab_f, lab_rel, lab_chip = lab.astype(F32), relative(lab), chip_of(lab)
    lab_t, chip_t = transposed(lab_f), transposed(lab_chip)
    earlier = one(iota((BLOCK, BLOCK), 0) < iota((BLOCK, BLOCK), 1))
    later = one(iota((BLOCK, BLOCK), 0) > iota((BLOCK, BLOCK), 1))
    slot = iota((SLOTS, BLOCK), 0).astype(F32)
    lane = iota((BLOCK, BLOCK), 1)
    most = jnp.zeros((1, 1), F32)
    slots = []
    for b in range(4):
        same = one(lab_t[:, b : b + 1] == lab_f[b : b + 1, :])
        same_chip = one(chip_t[:, b : b + 1] == lab_chip[b : b + 1, :])
        first_row = one(jnp.sum(same * earlier, axis=0, keepdims=True) == 0.0)
        first_col = one(jnp.sum(same * later, axis=1, keepdims=True) == 0.0)
        rank = jnp.sum(same_chip * earlier * first_col, axis=0, keepdims=True)
        most = jnp.maximum(most, jnp.max(rank * first_row, axis=1, keepdims=True) + 1.0)
        chosen = one(rank == slot) * (first_row * one(lab_chip[b : b + 1] == mine))
        slots.append(jnp.sum(chosen * (lab_rel[b : b + 1] + 1.0), axis=1, keepdims=True) - 1.0)
        if b == 0:
            rank_col = jnp.sum(same * (first_row * rank), axis=1, keepdims=True)
            chip = chip_t[:, 0:1].astype(I32)
            hop = (chip - y) & 3
            source = jnp.where(hop == 3, 2, jnp.where(hop == 2, 3, hop))
            arrival = (lax.shift_right_logical(chip, 2) * 4 + source) * SLOTS + rank_col.astype(I32)
            arrival = jnp.where(rank_col < SLOTS, arrival.astype(F32), -1.0)

    dec_chip, enc_chip = chip_of(dec), chip_of(enc)
    dec_rel, enc_rel = relative(dec), relative(enc)
    inside = jnp.concatenate([one(dec_chip == mine), one(enc_chip == mine)], axis=0)
    rank = jnp.dot(inside.astype(BF), earlier.astype(BF), preferred_element_type=F32)
    rank_enc = rank[8:16] + jnp.sum(inside[0:8], axis=1, keepdims=True)
    all_chips = iota((64, BLOCK), 0).astype(F32)
    tok_most = jnp.zeros((1, 1), F32)
    places = []
    for b in range(4):
        row = slice(b, b + 1)
        at = one(rank[row] == slot) * inside[row] * (dec_rel[row] + 1.0)
        at += one(rank_enc[row] == slot) * inside[8 + b : 9 + b] * (enc_rel[row] + 1.0)
        places.append(jnp.sum(at * one(slot < SLOTS - 1), axis=1, keepdims=True) - 1.0)
        count = one(dec_chip[row] == all_chips) + one(enc_chip[row] == all_chips)
        count = jnp.sum(count, axis=1, keepdims=True)
        tok_most = jnp.maximum(tok_most, jnp.max(count, axis=0, keepdims=True))
    cols = jnp.concatenate(slots + places, axis=0)
    cols = jnp.where(lane == 0, cols, jnp.where(lane == 1, most, jnp.where(lane == 2, tok_most, arrival)))
    rows_ref[...] = jnp.concatenate([lab_rel, cols.T[0:8]], axis=0)


def plan(ids):
    return small(
        plan_kernel,
        jax.ShapeDtypeStruct((16, BLOCK), F32),
        *ids,
    )


def by_lane(op, x):
    return functools.reduce(op, [x[:, 128 * i : 128 * (i + 1)] for i in range(x.shape[1] // 128)])


def logits_kernel(*refs):
    hidden = refs[:4]
    own_ref, sib_ref, number_ref, rows_ref = refs[4:8]
    own_out, sib_out, stats_ref = refs[9:12]
    payload = refs[12:16]
    states, table, logits, weights, in_sem, hidden_sem, out_sem = refs[16:]
    blocks = []
    for i in range(4):
        blocks.append(
            pltpu.make_async_copy(hidden[i], states.at[pl.ds(BLOCK * i, BLOCK)], hidden_sem.at[i])
        )
        blocks[i].start()
    loads = []
    for j in range(4):
        source = own_ref if j < 2 else sib_ref
        loads.append(
            pltpu.make_async_copy(
                source.at[pl.ds(CHUNK * (j % 2), CHUNK)], table.at[pl.ds(CHUNK * j, CHUNK)], in_sem.at[j]
            )
        )
        loads[j].start()
    for block in blocks:
        block.wait()

    cols = transposed(number_ref[0:8, :]).astype(I32)
    label = jnp.concatenate([cols[:, i : i + 1] for i in range(4)], axis=0)
    slot = transposed(number_ref[8:16, :])[0 : 4 * SLOTS, 0:1].astype(I32)
    stores = []
    peak = None
    for j in range(4):
        loads[j].wait()
        part = lax.dot_general(
            states[...], table[CHUNK * j : CHUNK * (j + 1), :], (((1,), (1,)), ((), ())), preferred_element_type=F32
        )
        logits[j] = part
        target = own_out if j < 2 else sib_out
        stores.append(pltpu.make_async_copy(logits.at[j], target.at[j % 2], out_sem.at[j]))
        stores[j].start()
        top = by_lane(jnp.maximum, part)
        peak = top if peak is None else jnp.maximum(peak, top)

    peak = jnp.max(peak, axis=1, keepdims=True)
    total = picked = None
    for j in range(4):
        part = logits[j]
        is_label = iota((NEAR, CHUNK), 1) + CHUNK * j == label
        weight = jnp.exp(part - peak)
        row_sum = by_lane(jnp.add, weight)
        hit = by_lane(jnp.add, jnp.where(is_label, part, 0.0))
        total = row_sum if total is None else total + row_sum
        picked = hit if picked is None else picked + hit
        at = slice(CHUNK * j, CHUNK * (j + 1))
        weights[0:NEAR, at] = jnp.where(is_label, 0.0, weight).astype(BF)
        slots = iota((4 * SLOTS, CHUNK), 1) + CHUNK * j == slot
        weights[NEAR:, at] = one(slots).astype(BF)

    total = jnp.sum(total, axis=1, keepdims=True)
    picked = jnp.sum(picked, axis=1, keepdims=True)
    lane = iota((NEAR, 128), 1)
    both = jnp.where(lane == 0, peak, jnp.where(lane == 1, total, jnp.where(lane == 2, picked, 0.0)))
    stats = both.T[0:8, :]
    stats_ref[...] = stats
    width = table.shape[1]
    left, digits = stats[0:1, :], []
    for _ in range(3):
        digits.append(left.astype(BF).astype(F32))
        left = left - digits[-1]
    for i in range(4):
        digit = [d[:, BLOCK * i : BLOCK * (i + 1)] for d in digits]
        digit = jnp.concatenate(digit + [jnp.zeros((1, width - 3 * BLOCK), F32)], axis=1)
        rows = rows_ref[SLOTS * i : SLOTS * (i + 1), :].astype(F32)
        payload[i][BLOCK + SLOTS : PAYLOAD, :] = jnp.where(
            iota((SLOTS, width), 0) == SLOTS - 1, digit, rows
        ).astype(BF)
    for j in range(4):
        at = slice(CHUNK * j, CHUNK * (j + 1))
        grad = jnp.dot(weights[...], table[:, at], preferred_element_type=F32).astype(BF)
        for i in range(4):
            payload[i][0:BLOCK, at] = grad[BLOCK * i : BLOCK * (i + 1)]
            payload[i][BLOCK : BLOCK + SLOTS, at] = grad[NEAR + SLOTS * i : NEAR + SLOTS * (i + 1)]
    for store in stores:
        store.wait()


def logits_and_grads(hidden, own, sib, numbers, rows, early):
    width = own.shape[1]
    anywhere = pl.BlockSpec(memory_space=pl.ANY)
    return pl.pallas_call(
        logits_kernel,
        in_specs=[anywhere] * 6 + [VMEM] * 2 + [anywhere],
        out_specs=[anywhere] * 2 + [VMEM] * 5,
        out_shape=[jax.ShapeDtypeStruct((2, NEAR, CHUNK), F32)] * 2
        + [jax.ShapeDtypeStruct((8, NEAR), F32)]
        + [jax.ShapeDtypeStruct((PAYLOAD, width), BF)] * 4,
        scratch_shapes=[
            pltpu.VMEM((NEAR, width), BF),
            pltpu.VMEM((2 * HALF, width), BF),
            pltpu.VMEM((4, NEAR, CHUNK), F32),
            pltpu.VMEM((NEAR + 4 * SLOTS, 2 * HALF), BF),
            pltpu.SemaphoreType.DMA((4,)),
            pltpu.SemaphoreType.DMA((4,)),
            pltpu.SemaphoreType.DMA((4,)),
        ],
        compiler_params=params(30 << 20),
    )(*hidden, own, sib, numbers, rows, *early)


def merged(parts):
    top = functools.reduce(jnp.maximum, [p[0:1] for p in parts])
    total = sum(p[1:2] * jnp.exp(p[0:1] - top) for p in parts)
    return top, total, sum(p[2:3] for p in parts)


def order_kernel(stats_ref, out_ref):
    _, y, _ = place()
    stats = stats_ref[...]
    for i in range(4):
        at = pl.multiple_of(lax.rem(y + HOPS[i], 4) * BLOCK, BLOCK)
        out_ref[:, pl.ds(at, BLOCK)] = stats[:, BLOCK * i : BLOCK * (i + 1)]


def merge_kernel(own_ref, other_ref, out_ref):
    own = own_ref[...]
    out_ref[...] = jnp.concatenate([*merged([own, other_ref[...]]), own[3:8]], axis=0)


def norm_kernel(own_ref, other_ref, row_ref, norm_ref, loss_ref, all_ref):
    _, y, _ = place()
    top, total, picked = merged([own_ref[...], other_ref[...]])
    norm = top + jnp.log(total)
    all_ref[...] = jnp.concatenate([norm, picked, jnp.zeros((6, NEAR), F32)], axis=0)

    def block(i):
        return all_ref[:, pl.ds(pl.multiple_of(lax.rem(y + HOPS[i], 4) * BLOCK, BLOCK), BLOCK)]

    mine = block(0)
    label = jnp.exp(mine[1:2] - mine[0:1]) - 1.0
    row_ref[...] = jnp.concatenate([mine[0:1], label, jnp.zeros((6, BLOCK), F32)], axis=0)
    loss_ref[...] = mine[0:1] - mine[1:2]
    norm_ref[...] = jnp.concatenate([block(i) for i in range(4)], axis=1)


def norms(stats):
    shape = jax.ShapeDtypeStruct((8, NEAR), F32)
    sums = small(order_kernel, shape, stats)
    for swap, step in ((swap_z, 0), (swap_z, 1), (swap_x, 0), (swap_x, 1), (swap_y, 0)):
        sums = small(merge_kernel, shape, sums, swap(sums, step))
    return small(
        norm_kernel,
        [
            jax.ShapeDtypeStruct((8, BLOCK), F32),
            jax.ShapeDtypeStruct((8, NEAR), F32),
            jax.ShapeDtypeStruct((1, BLOCK), F32),
        ],
        sums,
        swap_y(sums, 1),
        scratch=[pltpu.VMEM((8, NEAR), F32)],
    )


def combine_kernel(p0, p1, p2, p3, after_ref, parts_ref, rows_ref):
    payload = (p0, p1, p2, p3)
    peaks = []
    for i in range(4):
        rows = payload[i][BLOCK + SLOTS : PAYLOAD, :]
        rows_ref[SLOTS * i : SLOTS * (i + 1), :] = rows
        digits = rows[:, 0 : 3 * BLOCK].astype(F32)[SLOTS - 1 : SLOTS]
        peaks.append(digits[:, 2 * BLOCK :] + digits[:, BLOCK : 2 * BLOCK] + digits[:, 0:BLOCK])
    top = functools.reduce(jnp.maximum, peaks)
    cols = transposed(jnp.concatenate([jnp.exp(p - top) for p in peaks] + [jnp.zeros((4, BLOCK), F32)], axis=0))
    total = cols[:, 0:1] * payload[0][0:BLOCK, :].astype(F32)
    for i in range(1, 4):
        total += cols[:, i : i + 1] * payload[i][0:BLOCK, :].astype(F32)
    slots = jnp.concatenate([p[BLOCK : BLOCK + SLOTS, :] for p in payload], axis=0)
    left, digits = top, []
    for _ in range(3):
        digits.append(left.astype(BF).astype(F32))
        left = left - digits[-1]
    digits = jnp.concatenate(digits + [jnp.zeros((SLOTS - 3, BLOCK), F32)], axis=0).astype(BF)
    total = total.astype(BF)
    for i in range(parts_ref.shape[0]):
        at = slice(128 * i, 128 * (i + 1))
        parts_ref[i, 0:BLOCK, :] = total[:, at]
        parts_ref[i, BLOCK : BLOCK + 4 * SLOTS, :] = slots[:, at]
        parts_ref[i, BLOCK + 4 * SLOTS :, :] = digits


def combine(payload, after):
    width = payload[0].shape[1]
    return pl.pallas_call(
        combine_kernel,
        in_specs=[VMEM] * 5,
        out_specs=[VMEM] * 2,
        out_shape=[
            jax.ShapeDtypeStruct((16, BLOCK + 5 * SLOTS, width // 16), BF),
            jax.ShapeDtypeStruct((4 * SLOTS, width), BF),
        ],
        compiler_params=params(16 << 20),
    )(*payload, after)


def sum_kernel(groups_ref, row_ref, number_ref, end_ref, out_ref):
    count = groups_ref.shape[0]
    tail = BLOCK + 4 * SLOTS
    scales = []
    for i in range(count):
        digits = groups_ref[i, tail:, :].astype(F32)
        scales.append(jnp.exp(digits[2:3] + digits[1:2] + digits[0:1] - row_ref[0:1, :]))
    scales += [row_ref[1:2, :], number_ref[11:12, :], jnp.zeros((128 - count - 2, BLOCK), F32)]
    cols = jnp.concatenate(scales, axis=0).T
    slots = jnp.concatenate([groups_ref[i, BLOCK:tail, :] for i in range(count)], axis=0)
    at = cols[:, count + 1 : count + 2].astype(I32)
    chosen = one(iota((BLOCK, slots.shape[0]), 1) == at).astype(BF)
    total = cols[:, count : count + 1] * jnp.dot(chosen, slots, preferred_element_type=F32)
    for i in range(count):
        total += cols[:, i : i + 1] * groups_ref[i, 0:BLOCK, :].astype(F32)
    out_ref[...] = total + end_ref[0:1, :]


def table_kernel(*refs):
    logits, norms_of = refs[0:2], refs[2:4]
    numbers = refs[4:6]
    operands = refs[6:16]
    out_ref, end_ref, states, tiles, grads, results, logit_sem, state_sem, out_sem = refs[16:]
    count, _, tile = tiles.shape
    per = CHUNK // tile
    loads = [[], []]
    for j in range(count):
        for k in range(2):
            loads[k].append(
                pltpu.make_async_copy(
                    logits[k].at[j // per, :, pl.ds(tile * (j % per), tile)],
                    tiles.at[j, pl.ds(NEAR * k, NEAR)],
                    logit_sem.at[2 * j + k],
                )
            )
            loads[k][j].start()
    blocks = []
    low = 0
    for i, ref in enumerate(operands):
        rows = ref.shape[0]
        blocks.append(pltpu.make_async_copy(ref, states.at[pl.ds(low, rows)], state_sem.at[i]))
        blocks[i].start()
        low += rows

    norm = [transposed(ref[...])[:, 0:1] for ref in norms_of]
    labels, places = [], []
    for k in range(2):
        cols = transposed(numbers[k][0:8, :]).astype(I32)
        label = jnp.concatenate([cols[:, i : i + 1] for i in range(4)], axis=0)
        at = transposed(numbers[k][8:16, :])[4 * SLOTS : 8 * SLOTS, 0:1].astype(I32)
        labels.append(label ^ (HALF * k))
        places.append(jnp.where(at < 0, -1, at ^ (HALF * k)))
    places = jnp.concatenate(places, axis=0)

    def weigh(j):
        for k in range(2):
            at = slice(NEAR * k, NEAR * (k + 1))
            value = jnp.exp(tiles[j, at, :] - norm[k])
            is_label = iota((NEAR, tile), 1) + tile * j == labels[k]
            grads[j, at, :] = (value - one(is_label)).astype(BF)
        named = iota((8 * SLOTS, tile), 1) + tile * j == places
        grads[j, 2 * NEAR :, :] = one(named).astype(BF)

    end_ref[...] = jnp.zeros_like(end_ref)
    for k in range(2):
        loads[k][0].wait()
    weigh(0)
    for j in range(1, count):
        for k in range(2):
            loads[k][j].wait()
    for block in blocks:
        block.wait()
    stores = []
    for j in range(count):
        results[j] = lax.dot_general(
            grads[j], states[...], (((0,), (0,)), ((), ())), preferred_element_type=F32
        )
        stores.append(pltpu.make_async_copy(results.at[j], out_ref.at[pl.ds(tile * j, tile)], out_sem.at[j]))
        stores[j].start()
        if j + 1 < count:
            weigh(j + 1)
    for store in stores:
        store.wait()


def table_gradient(logits, norm_own, norm_sib, numbers, hidden, rows_own, rows_sib):
    width, tile = hidden[0].shape[1], 256
    count = HALF // tile
    rows = 2 * NEAR + 8 * SLOTS
    anywhere = pl.BlockSpec(memory_space=pl.ANY)
    return pl.pallas_call(
        table_kernel,
        in_specs=[anywhere] * 2 + [VMEM] * 4 + [anywhere] * 10,
        out_specs=[anywhere, VMEM],
        out_shape=[jax.ShapeDtypeStruct((HALF, width), F32), jax.ShapeDtypeStruct((8, 128), F32)],
        scratch_shapes=[
            pltpu.VMEM((rows, width), BF),
            pltpu.VMEM((count, 2 * NEAR, tile), F32),
            pltpu.VMEM((count, rows, tile), BF),
            pltpu.VMEM((count, tile, width), F32),
            pltpu.SemaphoreType.DMA((2 * count,)),
            pltpu.SemaphoreType.DMA((10,)),
            pltpu.SemaphoreType.DMA((count,)),
        ],
        compiler_params=params(),
    )(*logits, norm_own, norm_sib, *numbers, *hidden, rows_own, rows_sib)


def ranks(inside):
    n = inside.shape[-1]
    before = jnp.arange(n)[:, None] < jnp.arange(n)[None, :]
    return jnp.sum((inside[..., :, None] & before).astype(I32), axis=-2)


def pick(slot_of, inside, first_slot):
    slots = first_slot + jnp.arange(SLOTS, dtype=I32)
    return (slot_of[..., None, :] == slots[:, None]) & inside[..., None, :]


def exchange(rows):
    return [rows[0]] + [along_y(rows[BACK[i]], HOPS[i]) for i in range(1, 4)]


def more_label_rows(pairs, own_table, sib_table, first_slot):
    v, y, core = place()
    labels = jnp.stack([p[0] for p in pairs])
    chip = labels // (2 * HALF)
    same = labels[:, :, None] == labels[:, None, :]
    earlier = jnp.arange(BLOCK)[:, None] < jnp.arange(BLOCK)[None, :]
    is_first = ~jnp.any(same & earlier, axis=1)
    same_chip = chip[:, :, None] == chip[:, None, :]
    first_rank = jnp.sum((same_chip & earlier & is_first[:, :, None]).astype(I32), axis=1)
    rank = jnp.sum(jnp.where(same & is_first[:, :, None], first_rank[:, :, None], 0), axis=1)
    relative = (labels - (v * 4 + y) * (2 * HALF)) ^ (core * HALF)
    chosen = pick(rank, (chip == v * 4 + y) & is_first, first_slot)
    at = (jnp.sum(jnp.where(chosen, relative[:, None, :] + 1, 0), axis=2) - 1).reshape(4 * SLOTS, 1)
    row = jnp.arange(HALF, dtype=I32)
    rows = jnp.dot((at == row).astype(BF), own_table, preferred_element_type=F32)
    rows += jnp.dot((at == row + HALF).astype(BF), sib_table, preferred_element_type=F32)
    rows = rows.astype(BF).reshape(4, SLOTS, -1)
    got = jnp.concatenate(exchange([rows[i] for i in range(4)]))
    slot = jnp.arange(4 * SLOTS, dtype=I32)
    source = jnp.stack([v * 4 + (y + h) % 4 for h in HOPS])[slot // SLOTS]
    hit = (chip[0][:, None] == source[None]) & (rank[0][:, None] == (slot % SLOTS + first_slot)[None])
    return jnp.dot(hit.astype(BF), got, preferred_element_type=F32)


def more_token_rows(pairs, dec_grad, enc_grad, first_slot):
    v, y, core = place()
    own = jnp.concatenate([pairs[0][1], pairs[0][2]])
    chips = jnp.stack([v * 4 + (y + h) % 4 for h in HOPS])
    inside = own[None] // (2 * HALF) == chips[:, None]
    chosen = pick(ranks(inside), inside, first_slot).reshape(4 * SLOTS, 2 * BLOCK)
    rows = jnp.dot(chosen.astype(BF), jnp.concatenate([dec_grad, enc_grad]), preferred_element_type=F32)
    rows = rows.astype(BF).reshape(4, SLOTS, -1)
    got = jnp.concatenate(exchange([rows[i] for i in range(4)]))
    got = jnp.concatenate([got, sibling(got)])
    ids = jnp.stack(
        [jnp.concatenate([p[8 * c + 1], p[8 * c + 2]]) for c in range(2) for p in pairs]
    )
    inside = ids // (2 * HALF) == v * 4 + y
    chosen = pick(ranks(inside), inside, first_slot)
    relative = (ids - (v * 4 + y) * (2 * HALF)) ^ (core * HALF)
    at = jnp.sum(jnp.where(chosen, relative[:, None, :] + 1, 0), axis=2).reshape(1, 8 * SLOTS) - 1
    named = at == jnp.arange(HALF, dtype=I32)[:, None]
    return jnp.dot(named.astype(BF), got, preferred_element_type=F32)


def per_device(hidden_states, tied_table, labels, dec_ids, enc_ids, dec_grad, enc_grad):
    after, before = along_y(hidden_states, 1), along_y(hidden_states, -1)
    sib_table = sibling(tied_table)
    rows, own_ids = rows_to_send(labels, dec_ids, enc_ids, dec_grad, enc_grad)
    ids = [own_ids] + [along_y(own_ids, h) for h in HOPS[1:]]
    hidden = [hidden_states, after, before, farthest(after, before, ids[1:])]
    numbers = plan(ids)
    sib_numbers = sibling(numbers)
    hidden_sib = [sibling(h) for h in hidden]

    most = jnp.maximum(numbers[9:11, 0], sib_numbers[9:11, 0]).astype(I32)
    rounds_of_labels = (most[0] + SLOTS - 1) // SLOTS
    rounds_of_tokens = (most[1] + SLOTS) // SLOTS

    def all_ids(own):
        pair = jnp.concatenate([own, sibling(own)])
        return [pair] + [along_y(pair, h) for h in HOPS[1:]]

    own_logits, sib_logits, stats, *payload = logits_and_grads(
        hidden, tied_table, sib_table, numbers, rows, [sib_numbers]
    )

    payload = exchange(payload)
    mine, norm_rows, loss = norms(stats)

    got_logits = sibling(sib_logits)
    group, rows_own = combine(payload, mine)
    groups_of = lax.all_to_all(group, "vocab", 0, 0)

    grad_table, end = table_gradient(
        [own_logits, got_logits],
        norm_rows,
        sibling(norm_rows),
        [numbers, sib_numbers],
        hidden + hidden_sib,
        rows_own,
        sibling(rows_own),
    )

    grad_hidden = small(
        sum_kernel, jax.ShapeDtypeStruct((BLOCK, groups_of.shape[2]), F32), groups_of, mine, numbers, end
    )

    def add_labels(carry):
        r, grad = carry
        ids_r, slot = lax.optimization_barrier((own_ids, r * SLOTS))
        state = more_label_rows(all_ids(ids_r), tied_table, sib_table, slot).astype(BF)
        state = lax.all_to_all(state.reshape(BLOCK, 16, -1).transpose(1, 0, 2), "vocab", 0, 0)
        return r + 1, grad + mine[1][:, None] * jnp.sum(state.astype(F32), axis=0)

    _, grad_hidden = lax.while_loop(lambda c: c[0] < rounds_of_labels, add_labels, (jnp.int32(1), grad_hidden))

    def add_tokens(carry):
        r, grad = carry
        ids_r, dec, enc, slot = lax.optimization_barrier((own_ids, dec_grad, enc_grad, r * SLOTS - 1))
        return r + 1, grad + more_token_rows(all_ids(ids_r), dec, enc, slot)

    _, grad_table = lax.while_loop(lambda c: c[0] < rounds_of_tokens, add_tokens, (jnp.int32(1), grad_table))
    return grad_table, grad_hidden, loss.reshape(BLOCK)


def solution(mesh):
    in_specs = (
        P("tok", None),
        P(("vocab", "tok"), None),
        P("tok"),
        P("tok"),
        P("tok"),
        P("tok", None),
        P("tok", None),
    )
    out_specs = (P(("vocab", "tok"), None), P("tok", "vocab"), P("tok"))
    return jax.shard_map(
        per_device, mesh=mesh, in_specs=in_specs, out_specs=out_specs, check_vma=False
    )
```
